32 devices in a mesh: group: 2 (over y), gx: 16 (over z, x, core).
Axes of the slice: x: 2, y: 2, z: 4, core: 2. Of those that a mesh axis runs over, the one named last changes fastest.
Arguments:
- step_inputs: bfloat16 [2, 8, 8192], P(None, 'group'), parts along dimension 1, may hold values from -6 to 6
- mlp_inputs: bfloat16 [2, 8, 8192], P(None, 'group'), parts along dimension 1, may hold values from -6 to 6
- qkv_held: bfloat16 [10240, 8192], P('gx'), may hold values from -0.0625 to 0.0625
- gu_held: bfloat16 [28672, 8192], P('gx'), may hold values from -0.0625 to 0.0625
- old_owner: int32 [16], replicated, may hold values from 0 to 15, each once
- new_owner: int32 [16], replicated, may hold values from 0 to 15, each once
- kv_cache: bfloat16 [32768, 2048], P(('group', 'gx')), parts along dimension 0, may hold values from -500 to 500, as said below
- lengths: int32 [8], P('group'), parts along dimension 0, may hold values from 1 to 4096, as said below
Outputs:
- context: bfloat16 [2, 8, 8192], P(None, 'group'), parts along dimension 1
- activation: bfloat16 [2, 8, 14336], P(None, 'group'), parts along dimension 1
- qkv_tiles: bfloat16 [16384, 10240], P(('group', 'gx')), parts along dimension 0
- gu_tiles: bfloat16 [16384, 28672], P(('group', 'gx')), parts along dimension 0
The draws below stay inside these ranges and needn't reach their ends.
There are 2 independent parts, one for each index of `group`. The reference program is written for one: setup_inputs(seed, part) draws one part's arguments, and reference() takes and returns one part's arrays. A program takes and returns all parts, laid end to end along the dimension named above; an argument that names none is the same for every part. Nothing has to cross between parts.
Inputs may be any that keep to these rules, and one draw needn't show every extreme that they name: Request b's cached tokens are kv_cache rows b * 4096 + t for t < lengths[b]; some request holds all 4096. `kv_cache`: each row holds 8 key heads then 8 value heads of 128 entries.
All inputs are finite; a program needn't handle non-finite values.
Results may differ from the reference program's by a relative error of at most 0.03.
Values may be sent and summed in bfloat16 or wider, within the bound.
A program may use at most 320 MiB of HBM per device.

```python
import jax
import jax.numpy as jnp
from jax import lax

D = 8192
H = 64
KVH = 8
HD = 128
FF = 14336
CTX = 4096
ROWS = 4
QKV = 10240
N_GX = 16


def draw_kv_cache(key, part):
    key = jax.random.fold_in(key, 11)
    columns = 2 * KVH * HD
    pairs = ROWS * CTX // 2
    drawn_draw = jax.random.truncated_normal(key, -4.0, 4.0, (pairs, 2, columns), jnp.float32)
    spiked = jax.random.bernoulli(jax.random.fold_in(key, 1), 0.03, (pairs,))
    chosen_head = jax.random.randint(jax.random.fold_in(key, 2), (pairs,), 0, KVH)
    strength = jnp.exp(jax.random.uniform(jax.random.fold_in(key, 3), (pairs,), jnp.float32, jnp.log(40.0), jnp.log(160.0)))
    spread = jax.random.uniform(jax.random.fold_in(key, 4), (pairs,), jnp.float32, 0.005, 0.02)
    direction = jax.random.truncated_normal(jax.random.fold_in(key, 5), -3.0, 3.0, (pairs, HD), jnp.float32)
    tiled = jnp.tile(direction, (1, 2 * KVH))
    column_head = jnp.arange(columns) // HD
    in_head = column_head[None, :] == chosen_head[:, None]
    pair_scale = jnp.stack([strength, strength * (1.0 + spread)], axis=1)
    spike_rows = tiled[:, None, :] * pair_scale[:, :, None]
    use_spike = (spiked[:, None] & in_head)[:, None, :]
    drawn = jnp.where(use_spike, spike_rows, drawn_draw)
    return drawn.reshape(ROWS * CTX, columns).astype(jnp.bfloat16)


def draw_lengths(key, part):
    key = jax.random.fold_in(key, 23)
    drawn = jax.random.randint(key, (ROWS,), 1, CTX + 1)
    chosen = jax.random.randint(jax.random.fold_in(key, 5), (), 0, ROWS)
    return jnp.where(jnp.arange(ROWS) == chosen, CTX, drawn).astype(jnp.int32)


def shard_levels(key, shape, cuts, low, top_value):
    loudness = 1.0
    for dim, blocks in cuts:
        steps = jax.random.uniform(jax.random.fold_in(jax.random.fold_in(key, 6), dim), (blocks,), jnp.float32, low / len(cuts), top_value / len(cuts))
        loudness = loudness * jnp.repeat(jnp.exp(steps), shape[dim] // blocks).reshape((-1,) + (1,) * (len(shape) - 1 - dim))
    return loudness


def bell_draw(own_key, extent, width, limit, shards=(), dtype=jnp.bfloat16):
    values = width * jax.random.normal(own_key, extent, jnp.float32)
    if shards:
        values = values * shard_levels(own_key, extent, shards, -0.22, 0.18)
    return jnp.clip(values, -limit, limit).astype(dtype)


def setup_inputs(seed: int = 0, part: int = 0) -> dict:
    seeds = jax.random.split(jax.random.key(seed), 9)
    part_keys = jax.random.split(jax.random.fold_in(seeds[8], part), 9)
    step_inputs = bell_draw(part_keys[0], (2, ROWS, D), 1.0, 6.0)
    mlp_inputs = bell_draw(part_keys[1], (2, ROWS, D), 1.0, 6.0)
    qkv_held = bell_draw(seeds[2], (QKV, D), D ** -0.5, 0.0625, ((0, 16),))
    gu_held = bell_draw(seeds[3], (2 * FF, D), D ** -0.5, 0.0625, ((0, 16),))
    old_owner = jax.random.permutation(seeds[4], N_GX).astype(jnp.int32)
    new_owner = jax.random.permutation(seeds[5], N_GX).astype(jnp.int32)
    kv_cache = draw_kv_cache(jax.random.fold_in(jax.random.fold_in(seeds[8], part), 71), part)
    lengths = draw_lengths(jax.random.fold_in(jax.random.fold_in(seeds[8], part), 71), part)
    return {"step_inputs": step_inputs, "mlp_inputs": mlp_inputs, "qkv_held": qkv_held, "gu_held": gu_held, "old_owner": old_owner, "new_owner": new_owner, "kv_cache": kv_cache, "lengths": lengths}


very_negative = -1.0e30


def attend_row(packed):
    query_row, key_row, value_row, new_keys, new_values, length = packed
    score_scale = 1.0 / (HD ** 0.5)
    scores = jnp.einsum('sgqd,tgd->sgqt', query_row.astype(jnp.float32), key_row.astype(jnp.float32)) * score_scale
    valid = jnp.arange(CTX) < length
    scores = jnp.where(valid[None, None, None, :], scores, very_negative)
    new_scores = jnp.einsum('sgqd,jgd->sgqj', query_row.astype(jnp.float32), new_keys.astype(jnp.float32)) * score_scale
    causal = jnp.arange(2)[None, :] <= jnp.arange(2)[:, None]
    new_scores = jnp.where(causal[:, None, None, :], new_scores, very_negative)
    overall = jnp.maximum(jnp.max(scores, axis=3), jnp.max(new_scores, axis=3))
    weights = jnp.where(valid[None, None, None, :], jnp.exp(scores - overall[..., None]), 0.0)
    new_weights = jnp.where(causal[:, None, None, :], jnp.exp(new_scores - overall[..., None]), 0.0)
    total = jnp.sum(weights, axis=3) + jnp.sum(new_weights, axis=3)
    rounded = lax.optimization_barrier(weights.astype(jnp.bfloat16)).astype(jnp.float32)
    new_rounded = lax.optimization_barrier(new_weights.astype(jnp.bfloat16)).astype(jnp.float32)
    numer = jnp.einsum('sgqt,tgd->sgqd', rounded, value_row.astype(jnp.float32))
    numer = numer + jnp.einsum('sgqj,jgd->sgqd', new_rounded, new_values.astype(jnp.float32))
    return (numer / total[..., None]).astype(jnp.bfloat16).reshape(2, H * HD)


def reference(step_inputs, mlp_inputs, qkv_held, gu_held, old_owner, new_owner, kv_cache, lengths):
    new_inverse = jnp.argsort(new_owner).astype(jnp.int32)
    qkv_logical = qkv_held.reshape(N_GX, QKV // N_GX, D)[old_owner].reshape(QKV, D)
    gu_logical = gu_held.reshape(N_GX, 2 * FF // N_GX, D)[old_owner].reshape(2 * FF, D)
    qkv_tiles = qkv_logical.T.reshape(N_GX, D // N_GX, QKV)[new_inverse].reshape(D, QKV)
    gu_tiles = gu_logical.T.reshape(N_GX, D // N_GX, 2 * FF)[new_inverse].reshape(D, 2 * FF)
    projected = jnp.dot(step_inputs.reshape(2 * ROWS, D), qkv_logical.T, preferred_element_type=jnp.float32)
    projected = projected.astype(jnp.bfloat16).reshape(2, ROWS, QKV)
    gated = jnp.dot(mlp_inputs.reshape(2 * ROWS, D), gu_logical.T, preferred_element_type=jnp.float32)
    activation = (jax.nn.silu(gated[:, 0::2]) * gated[:, 1::2]).astype(jnp.bfloat16).reshape(2, ROWS, FF)
    group_size = H // KVH
    queries = projected[..., :H * HD].reshape(2, ROWS, KVH, group_size, HD)
    new_keys = projected[..., H * HD:(H + KVH) * HD].reshape(2, ROWS, KVH, HD)
    new_values = projected[..., (H + KVH) * HD:].reshape(2, ROWS, KVH, HD)
    cache = kv_cache.reshape(ROWS, CTX, 2, KVH, HD)
    packed = (jnp.moveaxis(queries, 1, 0), cache[:, :, 0], cache[:, :, 1],
              jnp.moveaxis(new_keys, 1, 0), jnp.moveaxis(new_values, 1, 0), lengths)
    context = jnp.moveaxis(lax.map(attend_row, packed), 0, 1)
    return context, activation, qkv_tiles, gu_tiles
```

```python
import functools

import jax
import jax.numpy as jnp
from jax import lax
from jax.experimental import pallas as pl
from jax.experimental.pallas import tpu as pltpu
from jax.sharding import PartitionSpec as P

H = 64
KVH = 8
HD = 128
CTX = 4096
ROWS = 4

very_negative = -1e30


def reorder_pieces(held, order, devices):
    height = held.shape[0]
    return held.reshape(height, devices, -1)[:, order, :].reshape(height, -1)


def settle_blocks(received, order, devices):
    height, breadth = received.shape
    placed = received.reshape(devices, height // devices, breadth)[order]
    return placed.reshape(height, breadth).T


def plain_tiles(held, new_inverse, old_owner, devices):
    sent = reorder_pieces(held, new_inverse, devices)
    received = lax.all_to_all(sent, "gx", split_axis=1, concat_axis=0, tiled=True)
    return settle_blocks(received, old_owner, devices)


def turn_kernel(columns, held_ref, out_ref):
    out_ref[0] = held_ref[...].T


def turn_pieces(held, columns, first, count, half):
    devices = columns.shape[0]
    return pl.pallas_call(
        turn_kernel,
        grid_spec=pltpu.PrefetchScalarGridSpec(
            num_scalar_prefetch=1,
            grid=(devices,),
            in_specs=[pl.BlockSpec((count, half), lambda p, columns: (first // count, columns[p]))],
            out_specs=pl.BlockSpec((1, half, count), lambda p, columns: (p, 0, 0)),
        ),
        out_shape=jax.ShapeDtypeStruct((devices, half, count), held.dtype),
        cost_estimate=pl.CostEstimate(
            flops=0, bytes_accessed=4 * devices * half * count, transcendentals=0
        ),
    )(columns, held)


def place_kernel(devices, half, height, first, count, order, which, *refs):
    source, tile, sems = refs[0], refs[-2], refs[-1]
    row = pl.multiple_of(which[0] * half, half)
    copies = []
    for c in range(devices):
        copy = pltpu.make_async_copy(
            source.at[order[c]],
            tile.at[pl.ds(row, half), pl.ds(c * height + first, count)],
            sems.at[c],
        )
        copy.start()
        copies.append(copy)
    for copy in copies:
        copy.wait()


def place_blocks(source, tile, order, which, height, first):
    devices, half, count = source.shape
    smem = pl.BlockSpec(memory_space=pltpu.SMEM)
    anywhere = pl.BlockSpec(memory_space=pl.ANY)
    operands = [order, which.reshape(1), source]
    aliases = {}
    if tile is not None:
        operands.append(tile)
        aliases = {3: 0}
    return pl.pallas_call(
        functools.partial(place_kernel, devices, half, height, first, count),
        out_shape=jax.ShapeDtypeStruct((2 * half, devices * height), source.dtype),
        in_specs=[smem, smem] + [anywhere] * (len(operands) - 2),
        out_specs=anywhere,
        scratch_shapes=[pltpu.SemaphoreType.DMA((devices,))],
        input_output_aliases=aliases,
        cost_estimate=pl.CostEstimate(
            flops=0, bytes_accessed=4 * devices * half * count, transcendentals=0
        ),
    )(*operands)


def shared_tiles(qkv_held, gu_held, new_inverse, old_owner, devices):
    mine = lax.axis_index("group")
    half = qkv_held.shape[1] // devices // 2
    columns = 2 * new_inverse.astype(jnp.int32) + mine
    chunks = [(1, 0, 512), (1, 512, 512), (1, 1024, 512), (0, 0, 512), (1, 1536, 256), (0, 512, 128)]
    held = (qkv_held, gu_held)
    tiles = [None, None]
    for which, first, count in chunks:
        sent = turn_pieces(held[which], columns, first, count, half)
        own = lax.all_to_all(sent, "gx", split_axis=0, concat_axis=0, tiled=True)
        other = lax.ppermute(own, "group", [(0, 1), (1, 0)])
        height = held[which].shape[0]
        tiles[which] = place_blocks(own, tiles[which], old_owner, mine, height, first)
        tiles[which] = place_blocks(other, tiles[which], old_owner, 1 - mine, height, first)
    return tiles


def gathered_columns(part, old_owner):
    steps, rows, width = part.shape
    blocks = lax.all_gather(part, "gx")[old_owner]
    return jnp.moveaxis(blocks, 0, 2).reshape(steps, rows, -1)


def local(step_inputs, mlp_inputs, qkv_held, gu_held, old_owner, new_owner, kv_cache, lengths):
    devices = lax.axis_size("gx")
    groups = lax.axis_size("group")
    myself = lax.axis_index("gx")
    in_block = qkv_held.shape[1] // devices
    new_inverse = jnp.argsort(new_owner)
    if groups == 2 and in_block == 512 and qkv_held.shape[0] == 640 and gu_held.shape[0] == 1792:
        qkv_tiles, gu_tiles = shared_tiles(qkv_held, gu_held, new_inverse, old_owner, devices)
    else:
        qkv_tiles = plain_tiles(qkv_held, new_inverse, old_owner, devices)
        gu_tiles = plain_tiles(gu_held, new_inverse, old_owner, devices)
    qkv_part = jnp.einsum("srd,cd->src", step_inputs, qkv_held, preferred_element_type=jnp.float32)
    projected = gathered_columns(qkv_part.astype(jnp.bfloat16), old_owner)
    gu_part = jnp.einsum("srd,cd->src", mlp_inputs, gu_held, preferred_element_type=jnp.float32)
    activated = (jax.nn.silu(gu_part[..., 0::2]) * gu_part[..., 1::2]).astype(jnp.bfloat16)
    activation = gathered_columns(activated, old_owner)
    score_scale = 1.0 / HD**0.5
    group_size = H // KVH
    local_tokens = kv_cache.shape[0]
    first_token = myself * local_tokens
    row_index = first_token // CTX
    offset = first_token % CTX
    queries = projected[..., : H * HD].reshape(2, ROWS, KVH, group_size, HD)
    new_keys = projected[..., H * HD : (H + KVH) * HD].reshape(2, ROWS, KVH, HD)
    new_values = projected[..., (H + KVH) * HD :].reshape(2, ROWS, KVH, HD)
    row_query = lax.dynamic_index_in_dim(queries, row_index, 1, keepdims=False)
    cache_keys = kv_cache[:, : KVH * HD].reshape(local_tokens, KVH, HD)
    cache_values = kv_cache[:, KVH * HD :].reshape(local_tokens, KVH, HD)
    scores = (
        jnp.einsum("sgqd,tgd->sgqt", row_query, cache_keys, preferred_element_type=jnp.float32)
        * score_scale
    )
    row_length = lax.dynamic_index_in_dim(lengths, row_index, 0, keepdims=False)
    valid = offset + jnp.arange(local_tokens, dtype=jnp.int32) < row_length
    scores = jnp.where(valid[None, None, None, :], scores, very_negative)
    local_top = jnp.max(scores, axis=3)
    weights = jnp.where(valid[None, None, None, :], jnp.exp(scores - local_top[..., None]), 0.0)
    local_total = jnp.sum(weights, axis=3)
    local_numer = jnp.einsum(
        "sgqt,tgd->sgqd",
        weights.astype(jnp.bfloat16),
        cache_values,
        preferred_element_type=jnp.float32,
    )
    shards = CTX // local_tokens
    pair_all = lax.all_gather(jnp.stack([local_top, local_total]), "gx")
    pair_all = pair_all.reshape(ROWS, shards, 2, 2, KVH, group_size)
    numer_parts = lax.all_gather(local_numer.astype(jnp.bfloat16), "gx")
    numer_parts = numer_parts.reshape(ROWS, shards, 2, KVH, group_size, HD)
    tops, totals = pair_all[:, :, 0], pair_all[:, :, 1]
    top_all = jnp.max(tops, axis=1)
    factors = jnp.exp(tops - top_all[:, None])
    total_all = jnp.moveaxis(jnp.sum(totals * factors, axis=1), 0, 1)
    numer_all = jnp.sum(numer_parts.astype(jnp.float32) * factors[..., None], axis=1)
    numer_all = jnp.moveaxis(numer_all, 0, 1)
    top_all = jnp.moveaxis(top_all, 0, 1)
    new_scores = (
        jnp.einsum("srgqd,jrgd->srgqj", queries, new_keys, preferred_element_type=jnp.float32)
        * score_scale
    )
    causal = jnp.arange(2)[None, :] <= jnp.arange(2)[:, None]
    causal_mask = causal[:, None, None, None, :]
    new_scores = jnp.where(causal_mask, new_scores, very_negative)
    overall = jnp.maximum(top_all, jnp.max(new_scores, axis=4))
    new_weights = jnp.where(causal_mask, jnp.exp(new_scores - overall[..., None]), 0.0)
    carried = jnp.exp(top_all - overall)
    total = total_all * carried + jnp.sum(new_weights, axis=4)
    numer = numer_all * carried[..., None]
    numer = numer + jnp.einsum(
        "srgqj,jrgd->srgqd",
        new_weights.astype(jnp.bfloat16),
        new_values,
        preferred_element_type=jnp.float32,
    )
    context = (numer / total[..., None]).astype(jnp.bfloat16).reshape(2, ROWS, H * HD)
    return (context, activation, qkv_tiles, gu_tiles)


def solution(mesh):
    return jax.shard_map(
        local,
        mesh=mesh,
        in_specs=(
            P(None, "group", None),
            P(None, "group", None),
            P("gx", None),
            P("gx", None),
            P(),
            P(),
            P(("group", "gx"), None),
            P("group"),
        ),
        out_specs=(
            P(None, "group", None),
            P(None, "group", None),
            P(("group", "gx"), None),
            P(("group", "gx"), None),
        ),
        check_vma=False,
    )
```

```python
import functools

import jax
import jax.numpy as jnp
from jax import lax
from jax.experimental import pallas as pl
from jax.experimental.pallas import tpu as pltpu
from jax.sharding import PartitionSpec as P

H = 64
KVH = 8
HD = 128
CTX = 4096
ROWS = 4

very_negative = -1e30


def reorder_pieces(held, order, devices):
    height = held.shape[0]
    return held.reshape(height, devices, -1)[:, order, :].reshape(height, -1)


def settle_blocks(received, order, devices):
    height, breadth = received.shape
    placed = received.reshape(devices, height // devices, breadth)[order]
    return placed.reshape(height, breadth).T


def plain_tiles(held, new_inverse, old_owner, devices):
    sent = reorder_pieces(held, new_inverse, devices)
    received = lax.all_to_all(sent, "gx", split_axis=1, concat_axis=0, tiled=True)
    return settle_blocks(received, old_owner, devices)


def turn_kernel(columns, held_ref, *refs):
    refs[-1][0] = held_ref[...].T


def turn_pieces(held, columns, first, count, half, after):
    devices = columns.shape[0]
    return pl.pallas_call(
        turn_kernel,
        grid_spec=pltpu.PrefetchScalarGridSpec(
            num_scalar_prefetch=1,
            grid=(devices,),
            in_specs=[pl.BlockSpec((count, half), lambda p, columns: (first // count, columns[p]))]
            + [pl.BlockSpec(memory_space=pl.ANY)] * len(after),
            out_specs=pl.BlockSpec((1, half, count), lambda p, columns: (p, 0, 0)),
        ),
        out_shape=jax.ShapeDtypeStruct((devices, half, count), held.dtype),
        cost_estimate=pl.CostEstimate(
            flops=0, bytes_accessed=4 * devices * half * count, transcendentals=0
        ),
    )(columns, held, *after)


def place_kernel(devices, half, height, first, count, order, which, *refs):
    source, (tile, token, buffer, in_sems, out_sems) = refs[0], refs[-5:]
    token[0] = 0
    row = pl.multiple_of(which[0] * half, half)
    loads, stores = [], []
    for c in range(devices):
        load = pltpu.make_async_copy(source.at[order[c]], buffer.at[c], in_sems.at[c])
        load.start()
        loads.append(load)
    for c in range(devices):
        loads[c].wait()
        store = pltpu.make_async_copy(
            buffer.at[c],
            tile.at[pl.ds(row, half), pl.ds(c * height + first, count)],
            out_sems.at[c],
        )
        store.start()
        stores.append(store)
    for store in stores:
        store.wait()


def place_blocks(source, tile, order, which, height, first):
    devices, half, count = source.shape
    smem = pl.BlockSpec(memory_space=pltpu.SMEM)
    anywhere = pl.BlockSpec(memory_space=pl.ANY)
    operands = [order, which.reshape(1), source]
    aliases = {}
    if tile is not None:
        operands.append(tile)
        aliases = {3: 0}
    return pl.pallas_call(
        functools.partial(place_kernel, devices, half, height, first, count),
        out_shape=(
            jax.ShapeDtypeStruct((2 * half, devices * height), source.dtype),
            jax.ShapeDtypeStruct((1,), jnp.int32),
        ),
        in_specs=[smem, smem] + [anywhere] * (len(operands) - 2),
        out_specs=(anywhere, smem),
        scratch_shapes=[
            pltpu.VMEM((devices, half, count), source.dtype),
            pltpu.SemaphoreType.DMA((devices,)),
            pltpu.SemaphoreType.DMA((devices,)),
        ],
        input_output_aliases=aliases,
        compiler_params=pltpu.CompilerParams(vmem_limit_bytes=24 * 2**20),
        cost_estimate=pl.CostEstimate(
            flops=0, bytes_accessed=4 * devices * half * count, transcendentals=0
        ),
    )(*operands)


def shared_tiles(qkv_held, gu_held, new_inverse, old_owner, devices, work):
    mine = lax.axis_index("group")
    half = qkv_held.shape[1] // devices // 2
    columns = 2 * new_inverse.astype(jnp.int32) + mine
    chunks = [(1, 0, 512), (1, 512, 512), (1, 1024, 512), (0, 0, 512), (1, 1536, 256), (0, 512, 128)]
    held = (qkv_held, gu_held)
    tiles = [None, None]
    tokens = []
    for k, (which, first, count) in enumerate(chunks):
        after = list(work[k]) + (tokens[k - 3] if k >= 3 else [])
        sent = turn_pieces(held[which], columns, first, count, half, after)
        own = lax.all_to_all(sent, "gx", split_axis=0, concat_axis=0, tiled=True)
        other = lax.ppermute(own, "group", [(0, 1), (1, 0)])
        height = held[which].shape[0]
        tile, token = place_blocks(own, tiles[which], old_owner, mine, height, first)
        tiles[which], later = place_blocks(other, tile, old_owner, 1 - mine, height, first)
        tokens.append([token, later])
    return tiles


def gathered_columns(part, old_owner):
    steps, rows, width = part.shape
    blocks = lax.all_gather(part, "gx")[old_owner]
    return jnp.moveaxis(blocks, 0, 2).reshape(steps, rows, -1)


def local(step_inputs, mlp_inputs, qkv_held, gu_held, old_owner, new_owner, kv_cache, lengths):
    devices = lax.axis_size("gx")
    groups = lax.axis_size("group")
    myself = lax.axis_index("gx")
    in_block = qkv_held.shape[1] // devices
    new_inverse = jnp.argsort(new_owner)
    qkv_part = jnp.einsum("srd,cd->src", step_inputs, qkv_held, preferred_element_type=jnp.float32)
    projected = gathered_columns(qkv_part.astype(jnp.bfloat16), old_owner)
    gu_part = jnp.einsum("srd,cd->src", mlp_inputs, gu_held, preferred_element_type=jnp.float32)
    activated = (jax.nn.silu(gu_part[..., 0::2]) * gu_part[..., 1::2]).astype(jnp.bfloat16)
    activation = gathered_columns(activated, old_owner)
    score_scale = 1.0 / HD**0.5
    group_size = H // KVH
    local_tokens = kv_cache.shape[0]
    first_token = myself * local_tokens
    row_index = first_token // CTX
    offset = first_token % CTX
    queries = projected[..., : H * HD].reshape(2, ROWS, KVH, group_size, HD)
    new_keys = projected[..., H * HD : (H + KVH) * HD].reshape(2, ROWS, KVH, HD)
    new_values = projected[..., (H + KVH) * HD :].reshape(2, ROWS, KVH, HD)
    row_query = lax.dynamic_index_in_dim(queries, row_index, 1, keepdims=False)
    cache_keys = kv_cache[:, : KVH * HD].reshape(local_tokens, KVH, HD)
    cache_values = kv_cache[:, KVH * HD :].reshape(local_tokens, KVH, HD)
    scores = (
        jnp.einsum("sgqd,tgd->sgqt", row_query, cache_keys, preferred_element_type=jnp.float32)
        * score_scale
    )
    row_length = lax.dynamic_index_in_dim(lengths, row_index, 0, keepdims=False)
    valid = offset + jnp.arange(local_tokens, dtype=jnp.int32) < row_length
    scores = jnp.where(valid[None, None, None, :], scores, very_negative)
    local_top = jnp.max(scores, axis=3)
    weights = jnp.where(valid[None, None, None, :], jnp.exp(scores - local_top[..., None]), 0.0)
    local_total = jnp.sum(weights, axis=3)
    local_numer = jnp.einsum(
        "sgqt,tgd->sgqd",
        weights.astype(jnp.bfloat16),
        cache_values,
        preferred_element_type=jnp.float32,
    )
    shards = CTX // local_tokens
    pair_all = lax.all_gather(jnp.stack([local_top, local_total]), "gx")
    pair_all = pair_all.reshape(ROWS, shards, 2, 2, KVH, group_size)
    numer_parts = lax.all_gather(local_numer.astype(jnp.bfloat16), "gx")
    numer_parts = numer_parts.reshape(ROWS, shards, 2, KVH, group_size, HD)
    tops, totals = pair_all[:, :, 0], pair_all[:, :, 1]
    top_all = jnp.max(tops, axis=1)
    factors = jnp.exp(tops - top_all[:, None])
    total_all = jnp.moveaxis(jnp.sum(totals * factors, axis=1), 0, 1)
    numer_all = jnp.sum(numer_parts.astype(jnp.float32) * factors[..., None], axis=1)
    numer_all = jnp.moveaxis(numer_all, 0, 1)
    top_all = jnp.moveaxis(top_all, 0, 1)
    new_scores = (
        jnp.einsum("srgqd,jrgd->srgqj", queries, new_keys, preferred_element_type=jnp.float32)
        * score_scale
    )
    causal = jnp.arange(2)[None, :] <= jnp.arange(2)[:, None]
    causal_mask = causal[:, None, None, None, :]
    new_scores = jnp.where(causal_mask, new_scores, very_negative)
    overall = jnp.maximum(top_all, jnp.max(new_scores, axis=4))
    new_weights = jnp.where(causal_mask, jnp.exp(new_scores - overall[..., None]), 0.0)
    carried = jnp.exp(top_all - overall)
    total = total_all * carried + jnp.sum(new_weights, axis=4)
    numer = numer_all * carried[..., None]
    numer = numer + jnp.einsum(
        "srgqj,jrgd->srgqd",
        new_weights.astype(jnp.bfloat16),
        new_values,
        preferred_element_type=jnp.float32,
    )
    context = (numer / total[..., None]).astype(jnp.bfloat16).reshape(2, ROWS, H * HD)
    if groups == 2 and in_block == 512 and qkv_held.shape[0] == 640 and gu_held.shape[0] == 1792:
        work = ((), (), (projected,), (activation,), (pair_all, numer_parts), (context,))
        qkv_tiles, gu_tiles = shared_tiles(
            qkv_held, gu_held, new_inverse, old_owner, devices, work
        )
    else:
        qkv_tiles = plain_tiles(qkv_held, new_inverse, old_owner, devices)
        gu_tiles = plain_tiles(gu_held, new_inverse, old_owner, devices)
    return (context, activation, qkv_tiles, gu_tiles)


def solution(mesh):
    return jax.shard_map(
        local,
        mesh=mesh,
        in_specs=(
            P(None, "group", None),
            P(None, "group", None),
            P("gx", None),
            P("gx", None),
            P(),
            P(),
            P(("group", "gx"), None),
            P("group"),
        ),
        out_specs=(
            P(None, "group", None),
            P(None, "group", None),
            P(("group", "gx"), None),
            P(("group", "gx"), None),
        ),
        check_vma=False,
    )
```

```python
import functools

import jax
import jax.numpy as jnp
from jax import lax
from jax.experimental import pallas as pl
from jax.experimental.pallas import tpu as pltpu
from jax.sharding import PartitionSpec as P

H = 64
KVH = 8
HD = 128
CTX = 4096
ROWS = 4

very_negative = -1e30


def reorder_pieces(held, order, devices):
    height = held.shape[0]
    return held.reshape(height, devices, -1)[:, order, :].reshape(height, -1)


def settle_blocks(received, order, devices):
    height, breadth = received.shape
    placed = received.reshape(devices, height // devices, breadth)[order]
    return placed.reshape(height, breadth).T


def plain_tiles(held, new_inverse, old_owner, devices):
    sent = reorder_pieces(held, new_inverse, devices)
    received = lax.all_to_all(sent, "gx", split_axis=1, concat_axis=0, tiled=True)
    return settle_blocks(received, old_owner, devices)


def turn_kernel(columns, held_ref, *refs):
    refs[-1][0] = held_ref[...].T


def turn_pieces(held, columns, first, count, half, after):
    devices = columns.shape[0]
    return pl.pallas_call(
        turn_kernel,
        grid_spec=pltpu.PrefetchScalarGridSpec(
            num_scalar_prefetch=1,
            grid=(devices,),
            in_specs=[pl.BlockSpec((count, half), lambda p, columns: (first // count, columns[p]))]
            + [pl.BlockSpec(memory_space=pl.ANY)] * len(after),
            out_specs=pl.BlockSpec((1, half, count), lambda p, columns: (p, 0, 0)),
        ),
        out_shape=jax.ShapeDtypeStruct((devices, half, count), held.dtype),
        cost_estimate=pl.CostEstimate(
            flops=0, bytes_accessed=4 * devices * half * count, transcendentals=0
        ),
    )(columns, held, *after)


def place_kernel(devices, half, height, first, count, order, which, *refs):
    source, (tile, token, buffer, in_sems, out_sems) = refs[0], refs[-5:]
    token[0] = 0
    row = pl.multiple_of(which[0] * half, half)
    loads, stores = [], []
    for c in range(devices):
        load = pltpu.make_async_copy(source.at[order[c]], buffer.at[c], in_sems.at[c])
        load.start()
        loads.append(load)
    for c in range(devices):
        loads[c].wait()
        store = pltpu.make_async_copy(
            buffer.at[c],
            tile.at[pl.ds(row, half), pl.ds(c * height + first, count)],
            out_sems.at[c],
        )
        store.start()
        stores.append(store)
    for store in stores:
        store.wait()


def place_blocks(source, tile, order, which, height, first, block):
    devices, half, count = source.shape
    smem = pl.BlockSpec(memory_space=pltpu.SMEM)
    anywhere = pl.BlockSpec(memory_space=pl.ANY)
    operands = [order, which.reshape(1), source]
    aliases = {}
    if tile is not None:
        operands.append(tile)
        aliases = {3: 0}
    return pl.pallas_call(
        functools.partial(place_kernel, devices, half, height, first, count),
        out_shape=(
            jax.ShapeDtypeStruct((block, devices * height), source.dtype),
            jax.ShapeDtypeStruct((1,), jnp.int32),
        ),
        in_specs=[smem, smem] + [anywhere] * (len(operands) - 2),
        out_specs=(anywhere, smem),
        scratch_shapes=[
            pltpu.VMEM((devices, half, count), source.dtype),
            pltpu.SemaphoreType.DMA((devices,)),
            pltpu.SemaphoreType.DMA((devices,)),
        ],
        input_output_aliases=aliases,
        compiler_params=pltpu.CompilerParams(vmem_limit_bytes=24 * 2**20),
        cost_estimate=pl.CostEstimate(
            flops=0, bytes_accessed=4 * devices * half * count, transcendentals=0
        ),
    )(*operands)


def hold_kernel(value_ref, *refs):
    refs[-1][...] = value_ref[...]


def hold(value, after):
    vmem = pl.BlockSpec(memory_space=pltpu.VMEM)
    return pl.pallas_call(
        hold_kernel,
        out_shape=jax.ShapeDtypeStruct(value.shape, value.dtype),
        in_specs=[vmem] + [pl.BlockSpec(memory_space=pl.ANY)] * len(after),
        out_specs=vmem,
    )(value, *after)


def three_parts(value):
    high = lax.reduce_precision(value, 8, 7)
    middle = lax.reduce_precision(value - high, 8, 7)
    low = value - high - middle
    return jnp.stack([high, middle, low]).astype(jnp.bfloat16)


chunks = (
    (1, 0, 512, True),
    (1, 512, 512, True),
    (1, 1024, 512, True),
    (0, 0, 512, True),
    (1, 1536, 256, True),
    (0, 512, 128, False),
)


class Retiling:
    def __init__(self, held, new_inverse, old_owner, devices):
        self.held, self.old_owner = held, old_owner
        self.inverse = new_inverse.astype(jnp.int32)
        self.mine = lax.axis_index("group")
        self.block = held[0].shape[1] // devices
        self.tiles = [None, None]
        self.sent, self.own, self.tokens = [], [], []

    def send(self, after):
        which, first, count, halves = chunks[len(self.sent)]
        held, mine = self.held[which], self.mine
        half = self.block // 2 if halves else self.block
        columns = 2 * self.inverse + mine if halves else self.inverse
        sent = turn_pieces(held, columns, first, count, half, after)
        own = lax.all_to_all(sent, "gx", split_axis=0, concat_axis=0, tiled=True)
        place = functools.partial(
            place_blocks, order=self.old_owner, height=held.shape[0], first=first, block=self.block
        )
        where = mine if halves else jnp.zeros((), jnp.int32)
        tile, token = place(own, self.tiles[which], which=where)
        tokens = [token]
        if halves:
            other = lax.ppermute(own, "group", [(0, 1), (1, 0)])
            tile, token = place(other, tile, which=1 - mine)
            tokens.append(token)
        self.tiles[which] = tile
        self.sent.append(sent)
        self.own.append(own)
        self.tokens.append(tokens)


def side_by_side(blocks, old_owner):
    _, steps, rows, _ = blocks.shape
    return jnp.moveaxis(blocks[old_owner], 0, 2).reshape(steps, rows, -1)


def local(step_inputs, mlp_inputs, qkv_held, gu_held, old_owner, new_owner, kv_cache, lengths):
    devices = lax.axis_size("gx")
    groups = lax.axis_size("group")
    myself = lax.axis_index("gx")
    in_block = qkv_held.shape[1] // devices
    new_inverse = jnp.argsort(new_owner)
    shared = (
        groups == 2 and in_block == 512 and qkv_held.shape[0] == 640 and gu_held.shape[0] == 1792
    )
    qkv_part = jnp.einsum("srd,cd->src", step_inputs, qkv_held, preferred_element_type=jnp.float32)
    gu_part = jnp.einsum("srd,cd->src", mlp_inputs, gu_held, preferred_element_type=jnp.float32)
    activated = (jax.nn.silu(gu_part[..., 0::2]) * gu_part[..., 1::2]).astype(jnp.bfloat16)
    parts = jnp.concatenate([qkv_part.astype(jnp.bfloat16), activated], axis=2)
    if shared:
        retiling = Retiling((qkv_held, gu_held), new_inverse, old_owner, devices)
        retiling.send(())
        retiling.send(())
        retiling.send((retiling.own[0],))
        parts = hold(parts, (retiling.sent[2],))
    part_blocks = lax.all_gather(parts, "gx")
    projected = side_by_side(part_blocks[..., : qkv_held.shape[0]], old_owner)
    activation = side_by_side(part_blocks[..., qkv_held.shape[0] :], old_owner)
    score_scale = 1.0 / HD**0.5
    group_size = H // KVH
    local_tokens = kv_cache.shape[0]
    first_token = myself * local_tokens
    row_index = first_token // CTX
    offset = first_token % CTX
    queries = projected[..., : H * HD].reshape(2, ROWS, KVH, group_size, HD)
    new_keys = projected[..., H * HD : (H + KVH) * HD].reshape(2, ROWS, KVH, HD)
    new_values = projected[..., (H + KVH) * HD :].reshape(2, ROWS, KVH, HD)
    row_query = lax.dynamic_index_in_dim(queries, row_index, 1, keepdims=False)
    cache_keys = kv_cache[:, : KVH * HD].reshape(local_tokens, KVH, HD)
    cache_values = kv_cache[:, KVH * HD :].reshape(local_tokens, KVH, HD)
    scores = (
        jnp.einsum("sgqd,tgd->sgqt", row_query, cache_keys, preferred_element_type=jnp.float32)
        * score_scale
    )
    row_length = lax.dynamic_index_in_dim(lengths, row_index, 0, keepdims=False)
    valid = offset + jnp.arange(local_tokens, dtype=jnp.int32) < row_length
    scores = jnp.where(valid[None, None, None, :], scores, very_negative)
    local_top = jnp.max(scores, axis=3)
    weights = jnp.where(valid[None, None, None, :], jnp.exp(scores - local_top[..., None]), 0.0)
    local_total = jnp.sum(weights, axis=3)
    local_numer = jnp.einsum(
        "sgqt,tgd->sgqd",
        weights.astype(jnp.bfloat16),
        cache_values,
        preferred_element_type=jnp.float32,
    )
    shards = CTX // local_tokens
    count = local_numer.size // HD
    packed = jnp.concatenate(
        [
            local_numer.astype(jnp.bfloat16).reshape(count, HD),
            three_parts(local_top).reshape(-1, HD),
            three_parts(local_total).reshape(-1, HD),
        ]
    )
    used = packed.shape[0]
    packed = jnp.pad(packed, ((0, -used % 16), (0, 0)))
    if shared:
        retiling.send((retiling.own[1],))
        packed = hold(packed, (retiling.sent[3],))
    everyone = lax.all_gather(packed, "gx")
    numer_parts = everyone[:, :count].reshape(ROWS, shards, 2, KVH, group_size, HD)
    pairs = everyone[:, count:used].astype(jnp.float32).reshape(devices, 2, 3, -1)
    pairs = (pairs[:, :, 0] + pairs[:, :, 1]) + pairs[:, :, 2]
    pairs = pairs.reshape(ROWS, shards, 2, 2, KVH, group_size)
    tops, totals = pairs[:, :, 0], pairs[:, :, 1]
    top_all = jnp.max(tops, axis=1)
    factors = jnp.exp(tops - top_all[:, None])
    total_all = jnp.moveaxis(jnp.sum(totals * factors, axis=1), 0, 1)
    numer_all = jnp.sum(numer_parts.astype(jnp.float32) * factors[..., None], axis=1)
    numer_all = jnp.moveaxis(numer_all, 0, 1)
    top_all = jnp.moveaxis(top_all, 0, 1)
    new_scores = (
        jnp.einsum("srgqd,jrgd->srgqj", queries, new_keys, preferred_element_type=jnp.float32)
        * score_scale
    )
    causal = jnp.arange(2)[None, :] <= jnp.arange(2)[:, None]
    causal_mask = causal[:, None, None, None, :]
    new_scores = jnp.where(causal_mask, new_scores, very_negative)
    overall = jnp.maximum(top_all, jnp.max(new_scores, axis=4))
    new_weights = jnp.where(causal_mask, jnp.exp(new_scores - overall[..., None]), 0.0)
    carried = jnp.exp(top_all - overall)
    total = total_all * carried + jnp.sum(new_weights, axis=4)
    numer = numer_all * carried[..., None]
    numer = numer + jnp.einsum(
        "srgqj,jrgd->srgqd",
        new_weights.astype(jnp.bfloat16),
        new_values,
        preferred_element_type=jnp.float32,
    )
    context = (numer / total[..., None]).astype(jnp.bfloat16).reshape(2, ROWS, H * HD)
    if shared:
        retiling.send((retiling.own[2], *retiling.tokens[0]))
        retiling.send((retiling.own[3], context, activation, *retiling.tokens[1]))
        qkv_tiles, gu_tiles = retiling.tiles
    else:
        qkv_tiles = plain_tiles(qkv_held, new_inverse, old_owner, devices)
        gu_tiles = plain_tiles(gu_held, new_inverse, old_owner, devices)
    return (context, activation, qkv_tiles, gu_tiles)


def solution(mesh):
    return jax.shard_map(
        local,
        mesh=mesh,
        in_specs=(
            P(None, "group", None),
            P(None, "group", None),
            P("gx", None),
            P("gx", None),
            P(),
            P(),
            P(("group", "gx"), None),
            P("group"),
        ),
        out_specs=(
            P(None, "group", None),
            P(None, "group", None),
            P(("group", "gx"), None),
            P(("group", "gx"), None),
        ),
        check_vma=False,
    )
```
